32 devices in a mesh: section: 2 (over core), dp: 4 (over z), tensor: 4 (over y, x).
Axes of the slice: x: 2, y: 2, z: 4, core: 2. Of those that a mesh axis runs over, the one named last changes fastest.
Arguments:
- block_input: bfloat16 [8, 384, 768], P('dp', 'tensor'), may hold values from -6 to 6
- cotangent: bfloat16 [8, 384, 768], P('dp', 'tensor'), may hold values from -6 to 6
- lengths: int32 [8], P('dp'), may hold values from 48 to 384, as said below
- qkv_weight: bfloat16 [2, 768, 3, 768], P('section', 'dp', None, 'tensor'), may hold values from -0.21875 to 0.21875
- qv_bias: float32 [2, 2, 768], P('section', None, 'tensor'), may hold values from -3 to 3
- out_weight: bfloat16 [2, 768, 768], P('section', 'tensor', 'dp'), may hold values from -1.25 to 1.25
- out_bias: float32 [2, 768], P('section'), may hold values from -3 to 3
- norm1_gain: float32 [2, 768], P('section'), may hold values from 0.25 to 1.75
- norm1_bias: float32 [2, 768], P('section'), may hold values from -2 to 2
- up_weight: bfloat16 [2, 768, 3072], P('section', 'dp', 'tensor'), may hold values from -0.21875 to 0.21875
- up_bias: float32 [2, 3072], P('section', 'tensor'), may hold values from -3 to 3
- down_weight: bfloat16 [2, 3072, 768], P('section', 'tensor', 'dp'), may hold values from -0.109375 to 0.109375
- down_bias: float32 [2, 768], P('section'), may hold values from -3 to 3
- norm2_gain: float32 [2, 768], P('section'), may hold values from 0.25 to 1.75
- norm2_bias: float32 [2, 768], P('section'), may hold values from -2 to 2
Outputs:
- block_output: bfloat16 [8, 384, 768], P('dp', 'tensor')
- input_grad: bfloat16 [8, 384, 768], P('dp', 'tensor', 'section')
- grad_qkv_weight: float32 [2, 768, 3, 768], P('section', 'dp', None, 'tensor')
- grad_qv_bias: float32 [2, 2, 768], P('section', None, ('tensor', 'dp'))
- grad_out_weight: float32 [2, 768, 768], P('section', 'tensor', 'dp')
- grad_out_bias: float32 [2, 768], P('section', ('dp', 'tensor'))
- grad_norm1_gain: float32 [2, 768], P('section', ('dp', 'tensor'))
- grad_norm1_bias: float32 [2, 768], P('section', ('dp', 'tensor'))
- grad_up_weight: float32 [2, 768, 3072], P('section', 'dp', 'tensor')
- grad_up_bias: float32 [2, 3072], P('section', ('tensor', 'dp'))
- grad_down_weight: float32 [2, 3072, 768], P('section', 'tensor', 'dp')
- grad_down_bias: float32 [2, 768], P('section', ('dp', 'tensor'))
- grad_norm2_gain: float32 [2, 768], P('section', ('dp', 'tensor'))
- grad_norm2_bias: float32 [2, 768], P('section', ('dp', 'tensor'))
The draws below stay inside these ranges and needn't reach their ends.
Inputs may be any that keep to these rules, and one draw needn't show every extreme that they name: `lengths`: each data group's 2 sequences include one of exactly 384 live tokens.
All inputs are finite; a program needn't handle non-finite values.
Results may differ from the reference program's by a relative error of at most 0.019.
Values may be sent and summed in bfloat16 or wider, within the bound.
A program may use at most 128 MiB of HBM per device.

```python
import jax
import jax.numpy as jnp
from jax import lax

D = 768
HEADS = 12
HEAD_DIM = 64
FF = 3072
SEQ = 384
MB = 2
NSEQ = 8
N_SECTION = 2


def draw_lengths(key, part):
    key = jax.random.fold_in(key, 11)
    first_key, second_key, third_key = jax.random.split(key, 3)
    groups = NSEQ // MB
    floor_len = jax.random.randint(first_key, (groups, 1), SEQ // 8, SEQ // 2 + 1)
    offsets = jax.random.randint(second_key, (groups, MB), 0, SEQ + 1)
    lengths = floor_len + offsets % (SEQ + 1 - floor_len)
    chosen = jax.random.randint(third_key, (groups, 1), 0, MB)
    lengths = jnp.where(jnp.arange(MB)[None, :] == chosen, SEQ, lengths)
    return lengths.reshape(NSEQ).astype(jnp.int32)


def steps_of(stream_key, extent, shards, smallest, top_value):
    level, own = 1.0, jax.random.fold_in(stream_key, 6)
    for axis_at, parts in shards:
        draws = jnp.exp(jax.random.uniform(jax.random.fold_in(own, axis_at), (parts,), jnp.float32, smallest / len(shards), top_value / len(shards)))
        level = level * jnp.repeat(draws, extent[axis_at] // parts).reshape([-1 if axis == axis_at else 1 for axis in range(len(extent))])
    return level


def scatter_about(stream_key, extent, spread, most, pieces=(), dtype=jnp.bfloat16):
    values = spread * jax.random.normal(stream_key, extent, jnp.float32)
    if pieces:
        values = values * steps_of(stream_key, extent, pieces, -0.22, 0.18)
    return jnp.clip(values, -most, most).astype(dtype)


def setup_inputs(seed: int = 0) -> dict:
    key_list = jax.random.split(jax.random.key(seed), 16)
    block_input = scatter_about(key_list[0], (NSEQ, SEQ, D), 1.0, 6.0, ((0, 4), (1, 4)))
    cotangent = scatter_about(key_list[1], (NSEQ, SEQ, D), 1.0, 6.0, ((0, 4), (1, 4)))
    lengths = draw_lengths(jax.random.fold_in(key_list[15], 71), 0)
    qkv_weight = scatter_about(key_list[3], (N_SECTION, D, 3, D), D ** -0.5, 0.21875, ((0, 2), (1, 4), (3, 4)))
    qv_bias = scatter_about(key_list[4], (N_SECTION, 2, D), 0.5, 3.0, ((0, 2), (2, 4)), jnp.float32)
    out_weight = scatter_about(key_list[5], (N_SECTION, D, D), (D // 32) ** -0.5, 1.25, ((0, 2), (1, 4), (2, 4)))
    out_bias = scatter_about(key_list[6], (N_SECTION, D), 0.5, 3.0, ((0, 2),), jnp.float32)
    norm1_gain = jnp.clip(1.0 + 0.15 * jax.random.normal(key_list[7], (N_SECTION, D), jnp.float32), 0.25, 1.75)
    norm1_bias = scatter_about(key_list[8], (N_SECTION, D), 0.3, 2.0, ((0, 2),), jnp.float32)
    up_weight = scatter_about(key_list[9], (N_SECTION, D, FF), D ** -0.5, 0.21875, ((0, 2), (1, 4), (2, 4)))
    up_bias = scatter_about(key_list[10], (N_SECTION, FF), 0.5, 3.0, ((0, 2), (1, 4)), jnp.float32)
    down_weight = scatter_about(key_list[11], (N_SECTION, FF, D), FF ** -0.5, 0.109375, ((0, 2), (1, 4), (2, 4)))
    down_bias = scatter_about(key_list[12], (N_SECTION, D), 0.5, 3.0, ((0, 2),), jnp.float32)
    norm2_gain = jnp.clip(1.0 + 0.15 * jax.random.normal(key_list[13], (N_SECTION, D), jnp.float32), 0.25, 1.75)
    norm2_bias = scatter_about(key_list[14], (N_SECTION, D), 0.3, 2.0, ((0, 2),), jnp.float32)
    return {"block_input": block_input, "cotangent": cotangent, "lengths": lengths, "qkv_weight": qkv_weight, "qv_bias": qv_bias, "out_weight": out_weight, "out_bias": out_bias, "norm1_gain": norm1_gain, "norm1_bias": norm1_bias, "up_weight": up_weight, "up_bias": up_bias, "down_weight": down_weight, "down_bias": down_bias, "norm2_gain": norm2_gain, "norm2_bias": norm2_bias}


@jax.custom_vjp
def low(v):
    return lax.optimization_barrier(v.astype(jnp.bfloat16)).astype(jnp.float32)

@jax.custom_vjp
def low_back(v):
    return v

def low_keep(v):
    return (low(v), None)

def low_pass(kept, grad):
    return (grad,)

def back_keep(v):
    return (v, None)

def back_low(kept, grad):
    return (low(grad),)
low.defvjp(low_keep, low_pass)
low_back.defvjp(back_keep, back_low)
norm_epsilon = 1e-05
masked_score = -1e+30

def exact_dot(left, right):
    return jnp.dot(left, right, precision=lax.Precision.HIGHEST)

def layer_norm(summed, gain, shift):
    centre = lax.optimization_barrier(jnp.mean(summed, axis=-1, keepdims=True))
    centred = summed - centre
    variance = lax.optimization_barrier(jnp.mean(centred * centred, axis=-1, keepdims=True))
    return centred * lax.rsqrt(variance + norm_epsilon) * gain + shift

def encoder_layer(params, inputs, length):
    qkv_weight, qv_bias, out_weight, out_bias, norm1_gain, norm1_bias, up_weight, up_bias, down_weight, down_bias, norm2_gain, norm2_bias = params
    seq_len = inputs.shape[0]
    source = low(inputs)
    pre_proj = exact_dot(source, qkv_weight.reshape(D, 3 * D)).reshape(seq_len, 3, D)
    qkv_bias = jnp.stack([qv_bias[0], jnp.zeros((D,), jnp.float32), qv_bias[1]])
    projected = low_back(low(pre_proj + qkv_bias))
    split_heads = projected.reshape(seq_len, 3, HEADS, HEAD_DIM)
    queries = split_heads[:, 0]
    key_rows = split_heads[:, 1]
    values = split_heads[:, 2]
    score_scale = HEAD_DIM ** (-0.5)
    raw_scores = jnp.einsum('qhd,khd->hqk', queries, key_rows, precision=lax.Precision.HIGHEST) * score_scale
    raw_scores = low_back(raw_scores)
    key_live = jnp.arange(seq_len) < length
    raw_scores = jnp.where(key_live[None, None, :], raw_scores, masked_score)
    row_max = lax.optimization_barrier(jnp.max(raw_scores, axis=-1, keepdims=True))
    exponent = jnp.exp(raw_scores - row_max)
    attn_probs = exponent / lax.optimization_barrier(jnp.sum(exponent, axis=-1, keepdims=True))
    context = jnp.einsum('hqk,khd->qhd', low(attn_probs), values, precision=lax.Precision.HIGHEST)
    context = low_back(low(context.reshape(seq_len, D)))
    attended = low_back(exact_dot(context, out_weight)) + out_bias
    normed = layer_norm(inputs + attended, norm1_gain, norm1_bias)
    hidden_pre = low_back(exact_dot(low(normed), up_weight) + up_bias)
    hidden = low(jax.nn.gelu(hidden_pre, approximate=False))
    mlp_out = low_back(exact_dot(hidden, down_weight)) + down_bias
    return layer_norm(normed + mlp_out, norm2_gain, norm2_bias)

def section_params(weights, section_number):
    return tuple((member[section_number] for member in weights))

def reference(block_input, cotangent, lengths, qkv_weight, qv_bias, out_weight, out_bias, norm1_gain, norm1_bias, up_weight, up_bias, down_weight, down_bias, norm2_gain, norm2_bias):
    weights = tuple((member.astype(jnp.float32) for member in (qkv_weight, qv_bias, out_weight, out_bias, norm1_gain, norm1_bias, up_weight, up_bias, down_weight, down_bias, norm2_gain, norm2_bias)))
    inputs = block_input.astype(jnp.float32)
    group_limit = max(1, 4096 // SEQ)
    group_size = max((divisor for divisor in range(1, group_limit + 1) if NSEQ % divisor == 0))

    def full_forward(inputs, weights):
        first_params = section_params(weights, 0)
        second_params = section_params(weights, 1)

        def one_sequence(seq_in, length):
            middle = encoder_layer(first_params, seq_in, length)
            return encoder_layer(second_params, middle, length)
        block_fn = jax.checkpoint(lambda block_pair: jax.vmap(one_sequence)(block_pair[0], block_pair[1]))
        blocks = (inputs.reshape(NSEQ // group_size, group_size, SEQ, D), lengths.reshape(NSEQ // group_size, group_size))
        return lax.map(block_fn, blocks).reshape(NSEQ, SEQ, D)
    result, pull_back = jax.vjp(full_forward, inputs, weights)
    row_live = (jnp.arange(SEQ)[None, :] < lengths[:, None]).astype(jnp.float32)
    cot_masked = cotangent.astype(jnp.float32) * row_live[:, :, None]
    input_grad, weight_grads = pull_back(cot_masked)
    return (result.astype(jnp.bfloat16), input_grad.astype(jnp.bfloat16), weight_grads[0], weight_grads[1], weight_grads[2], weight_grads[3], weight_grads[4], weight_grads[5], weight_grads[6], weight_grads[7], weight_grads[8], weight_grads[9], weight_grads[10], weight_grads[11])
```

```python
import functools

import jax
import jax.numpy as jnp
from jax import lax
from jax.experimental import pallas as pl
from jax.experimental.pallas import tpu as pltpu
from jax.sharding import PartitionSpec as P

HEAD_DIM = 64


masked_score = -1e30
norm_epsilon = 1e-05


def meet_peers(axis):
    me = lax.axis_index(axis)
    count = lax.axis_size(axis)
    barrier = pltpu.get_barrier_semaphore()
    for step in range(1, count):
        pl.semaphore_signal(
            barrier,
            inc=1,
            device_id={axis: lax.rem(me + step, count)},
            device_id_type=pl.DeviceIdType.MESH,
        )
    pl.semaphore_wait(barrier, count - 1)


def gather_kernel(axis, tile_ref, out_ref, send_sem, recv_sem):
    me = lax.axis_index(axis)
    count = lax.axis_size(axis)
    meet_peers(axis)
    copies = []
    for step in range(1, count):
        copy = pltpu.make_async_remote_copy(
            src_ref=tile_ref,
            dst_ref=out_ref.at[me],
            send_sem=send_sem.at[step],
            recv_sem=recv_sem.at[step],
            device_id={axis: lax.rem(me + step, count)},
            device_id_type=pl.DeviceIdType.MESH,
        )
        copy.start()
        copies.append(copy)
    out_ref[me] = tile_ref[...]
    for copy in copies:
        copy.wait()


def reduce_kernel(axis, partial_ref, out_ref, staged, landed, send_sem, recv_sem):
    me = lax.axis_index(axis)
    count = lax.axis_size(axis)
    staged[...] = partial_ref[...].astype(jnp.bfloat16)
    meet_peers(axis)
    copies = []
    for step in range(1, count):
        peer = lax.rem(me + step, count)
        copy = pltpu.make_async_remote_copy(
            src_ref=staged.at[peer],
            dst_ref=landed.at[step],
            send_sem=send_sem.at[step],
            recv_sem=recv_sem.at[step],
            device_id={axis: peer},
            device_id_type=pl.DeviceIdType.MESH,
        )
        copy.start()
        copies.append(copy)
    total = partial_ref[me]
    for step, copy in enumerate(copies):
        copy.wait()
        total = total + landed[step + 1].astype(jnp.float32)
    out_ref[...] = total


def gather_rows(tile):
    count = lax.axis_size("tensor")
    rows, width = tile.shape
    gathered = pl.pallas_call(
        functools.partial(gather_kernel, "tensor"),
        out_shape=jax.ShapeDtypeStruct((count, rows, width), tile.dtype),
        in_specs=[pl.BlockSpec(memory_space=pltpu.VMEM)],
        out_specs=pl.BlockSpec(memory_space=pltpu.VMEM),
        scratch_shapes=[
            pltpu.SemaphoreType.DMA((count,)),
            pltpu.SemaphoreType.DMA((count,)),
        ],
        compiler_params=pltpu.CompilerParams(
            collective_id=0, has_side_effects=True, vmem_limit_bytes=32 * 1024 * 1024
        ),
    )(tile)
    return gathered.reshape(count * rows, width)


def reduce_rows(partial_value):
    count = lax.axis_size("tensor")
    rows, width = partial_value.shape
    rows = rows // count
    return pl.pallas_call(
        functools.partial(reduce_kernel, "tensor"),
        out_shape=jax.ShapeDtypeStruct((rows, width), jnp.float32),
        in_specs=[pl.BlockSpec(memory_space=pltpu.VMEM)],
        out_specs=pl.BlockSpec(memory_space=pltpu.VMEM),
        scratch_shapes=[
            pltpu.VMEM((count, rows, width), jnp.bfloat16),
            pltpu.VMEM((count, rows, width), jnp.bfloat16),
            pltpu.SemaphoreType.DMA((count,)),
            pltpu.SemaphoreType.DMA((count,)),
        ],
        compiler_params=pltpu.CompilerParams(
            collective_id=1, has_side_effects=True, vmem_limit_bytes=32 * 1024 * 1024
        ),
    )(partial_value.reshape(count, rows, width))


gather_grads = gather_rows
reduce_grads = reduce_rows


def norm_forward(summed, gain, shift):
    centre = jnp.mean(summed, axis=-1, keepdims=True)
    centred = summed - centre
    inverse = lax.rsqrt(jnp.mean(centred * centred, axis=-1, keepdims=True) + norm_epsilon)
    scaled = centred * inverse
    return (scaled * gain + shift, scaled, inverse)


def norm_backward(upstream, scaled, inverse, gain):
    weighted = upstream * gain
    inner_sum = jnp.mean(weighted, axis=-1, keepdims=True)
    along_sum = jnp.mean(weighted * scaled, axis=-1, keepdims=True)
    return (
        inverse * (weighted - inner_sum - scaled * along_sum),
        jnp.sum(upstream * scaled, axis=0),
        jnp.sum(upstream, axis=0),
    )


def gelu_slope(hidden_pre):
    cumulative = 0.5 * (1.0 + lax.erf(hidden_pre * 0.7071067811865476))
    density = jnp.exp(-0.5 * hidden_pre * hidden_pre) * 0.3989422804014327
    return cumulative + hidden_pre * density


def masked_scores(queries, key_rows, length, score_scale):
    raw_scores = (
        jnp.einsum("qhd,khd->hqk", queries, key_rows, preferred_element_type=jnp.float32)
        * score_scale
    )
    key_live = jnp.arange(key_rows.shape[0]) < length
    return jnp.where(key_live[None, None, :], raw_scores, masked_score)


def layer_forward(incoming, full_weights, small_params, length):
    up_full, down_turned, qkv_full, out_turned = full_weights
    qv_bias, out_bias, gain_one, shift_one, up_bias, down_bias, gain_two, shift_two = small_params
    gathered = gather_rows(incoming.astype(jnp.bfloat16))
    seq_len, model_width = gathered.shape
    local_width = out_turned.shape[-1]
    head_count = local_width // HEAD_DIM
    score_scale = HEAD_DIM ** (-0.5)
    pre_proj = jnp.dot(
        gathered, qkv_full, preferred_element_type=jnp.float32
    )
    qkv_bias = jnp.stack([qv_bias[0], jnp.zeros_like(qv_bias[0]), qv_bias[1]]).reshape(
        3 * local_width
    )
    projected = (pre_proj + qkv_bias).astype(jnp.bfloat16).reshape(seq_len, 3, head_count, HEAD_DIM)
    raw_scores = masked_scores(projected[:, 0], projected[:, 1], length, score_scale)
    row_max = jnp.max(raw_scores, axis=-1, keepdims=True)
    exponent = jnp.exp(raw_scores - row_max)
    row_total = jnp.sum(exponent, axis=-1, keepdims=True)
    attn_probs = (exponent / row_total).astype(jnp.bfloat16)
    log_total = row_max + jnp.log(row_total)
    context = jnp.einsum(
        "hqk,khd->qhd", attn_probs, projected[:, 2], preferred_element_type=jnp.float32
    )
    context = context.reshape(seq_len, local_width).astype(jnp.bfloat16)
    attended = reduce_rows(jnp.einsum("sc,dc->sd", context, out_turned, preferred_element_type=jnp.float32))
    first_sum = incoming + attended + out_bias
    normed, scaled_one, inverse_one = norm_forward(first_sum, gain_one, shift_one)
    normed_rows = gather_rows(normed.astype(jnp.bfloat16))
    hidden_pre = jnp.dot(normed_rows, up_full, preferred_element_type=jnp.float32) + up_bias
    hidden = jax.nn.gelu(hidden_pre, approximate=False).astype(jnp.bfloat16)
    mlp_out = reduce_rows(jnp.einsum("sf,df->sd", hidden, down_turned, preferred_element_type=jnp.float32))
    second_sum = normed + mlp_out + down_bias
    result, scaled_two, inverse_two = norm_forward(second_sum, gain_two, shift_two)
    saved_acts = (
        gathered,
        projected,
        log_total,
        context,
        scaled_one,
        inverse_one,
        normed_rows,
        hidden_pre,
        hidden,
        scaled_two,
        inverse_two,
    )
    return (result, saved_acts)


def layer_backward(upstream, saved_acts, full_weights, small_params, length):
    (
        gathered,
        projected,
        log_total,
        context,
        scaled_one,
        inverse_one,
        normed_rows,
        hidden_pre,
        hidden,
        scaled_two,
        inverse_two,
    ) = saved_acts
    up_full, down_turned, qkv_full, out_turned = full_weights
    qv_bias, out_bias, gain_one, shift_one, up_bias, down_bias, gain_two, shift_two = small_params
    seq_len, model_width = gathered.shape
    local_width = out_turned.shape[-1]
    head_count = local_width // HEAD_DIM
    score_scale = HEAD_DIM ** (-0.5)
    second_grad, gain_two_grad, shift_two_grad = norm_backward(
        upstream, scaled_two, inverse_two, gain_two
    )
    down_bias_grad = jnp.sum(second_grad, axis=0)
    mixed_rows = gather_grads(second_grad.astype(jnp.bfloat16))
    down_grad = jnp.einsum("sf,sd->df", hidden, mixed_rows, preferred_element_type=jnp.float32)
    hidden_grad = jnp.einsum("sd,df->sf", mixed_rows, down_turned, preferred_element_type=jnp.float32)
    pre_grad = (hidden_grad * gelu_slope(hidden_pre)).astype(jnp.bfloat16)
    up_bias_grad = jnp.sum(pre_grad.astype(jnp.float32), axis=0)
    up_grad = jnp.einsum("sd,sf->df", normed_rows, pre_grad, preferred_element_type=jnp.float32)
    normed_grad = second_grad + reduce_grads(
        jnp.einsum("sf,df->sd", pre_grad, up_full, preferred_element_type=jnp.float32)
    )
    first_grad, gain_one_grad, shift_one_grad = norm_backward(
        normed_grad, scaled_one, inverse_one, gain_one
    )
    out_bias_grad = jnp.sum(first_grad, axis=0)
    attended_rows = gather_grads(first_grad.astype(jnp.bfloat16))
    out_grad = jnp.einsum("sc,sd->dc", context, attended_rows, preferred_element_type=jnp.float32)
    context_grad = jnp.einsum(
        "sd,dc->sc", attended_rows, out_turned, preferred_element_type=jnp.float32
    )
    context_grad = context_grad.astype(jnp.bfloat16).reshape(seq_len, head_count, HEAD_DIM)
    queries = projected[:, 0]
    key_rows = projected[:, 1]
    values = projected[:, 2]
    attn_probs = jnp.exp(masked_scores(queries, key_rows, length, score_scale) - log_total)
    value_grad = jnp.einsum(
        "hqk,qhd->khd",
        attn_probs.astype(jnp.bfloat16),
        context_grad,
        preferred_element_type=jnp.float32,
    )
    probs_grad = jnp.einsum(
        "qhd,khd->hqk", context_grad, values, preferred_element_type=jnp.float32
    )
    inner_sum = jnp.sum(attn_probs * probs_grad, axis=-1, keepdims=True)
    score_grad = (attn_probs * (probs_grad - inner_sum)).astype(jnp.bfloat16)
    query_grad = (
        jnp.einsum("hqk,khd->qhd", score_grad, key_rows, preferred_element_type=jnp.float32)
        * score_scale
    )
    key_grad = (
        jnp.einsum("hqk,qhd->khd", score_grad, queries, preferred_element_type=jnp.float32)
        * score_scale
    )
    proj_grad = (
        jnp.stack([query_grad, key_grad, value_grad], axis=1)
        .astype(jnp.bfloat16)
        .reshape(seq_len, 3 * local_width)
    )
    summed_proj = jnp.sum(proj_grad.astype(jnp.float32).reshape(seq_len, 3, local_width), axis=0)
    qv_bias_grad = jnp.stack([summed_proj[0], summed_proj[2]])
    qkv_grad = jnp.einsum(
        "sd,sx->dx", gathered, proj_grad, preferred_element_type=jnp.float32
    )
    input_part = jnp.einsum(
        "sx,dx->sd",
        proj_grad,
        qkv_full,
        preferred_element_type=jnp.float32,
    )
    input_grad = first_grad + reduce_grads(input_part)
    matrix = jnp.concatenate([up_grad, down_grad, qkv_grad, out_grad], axis=1).astype(jnp.bfloat16)
    columns = jnp.concatenate([qv_bias_grad.reshape(-1), up_bias_grad])
    rowwise = (
        out_bias_grad,
        gain_one_grad,
        shift_one_grad,
        down_bias_grad,
        gain_two_grad,
        shift_two_grad,
    )
    return (input_grad, matrix, columns, jnp.concatenate(rowwise))


def local(
    block_input,
    cotangent,
    lengths,
    qkv_weight,
    qv_bias,
    out_weight,
    out_bias,
    norm1_gain,
    norm1_bias,
    up_weight,
    up_bias,
    down_weight,
    down_bias,
    norm2_gain,
    norm2_bias,
):
    section_index = lax.axis_index("section")
    tensor_index = lax.axis_index("tensor")
    dp_index = lax.axis_index("dp")
    dp_count = lax.axis_size("dp")
    layer_count = lax.axis_size("section")
    row_count = block_input.shape[1]
    model_width = block_input.shape[2]
    head_width = out_weight.shape[1]
    hidden_width = up_weight.shape[2]
    length = lengths[section_index]
    row_live = tensor_index * row_count + jnp.arange(row_count) < length
    packed = jnp.concatenate(
        [
            up_weight[0],
            down_weight[0].T,
            qkv_weight[0].reshape(qkv_weight.shape[1], 3 * head_width),
            out_weight[0].T,
        ],
        axis=1,
    )
    cuts = [hidden_width, 2 * hidden_width, 2 * hidden_width + 3 * head_width]
    packed_full = lax.all_gather(packed, ("section", "dp"), axis=0, tiled=True)
    small = (qv_bias, out_bias, norm1_gain, norm1_bias, up_bias, down_bias, norm2_gain, norm2_bias)
    small_flat = jnp.concatenate([member.reshape(-1) for member in small])
    small_both = lax.all_gather(small_flat, "section", axis=0)
    layer_weights = []
    layer_small = []
    for layer in range(layer_count):
        whole = packed_full[layer * model_width : (layer + 1) * model_width]
        layer_weights.append(jnp.split(whole, cuts, axis=1))
        start = 0
        members = []
        for member in small:
            members.append(small_both[layer, start : start + member.size].reshape(member.shape[1:]))
            start += member.size
        layer_small.append(tuple(members))
    running = lax.dynamic_index_in_dim(block_input, section_index, 0, keepdims=False).astype(
        jnp.float32
    )
    saved = []
    for layer in range(layer_count):
        running, acts = layer_forward(running, layer_weights[layer], layer_small[layer], length)
        saved.append(acts)
    upstream = (
        lax.dynamic_index_in_dim(cotangent, section_index, 0, keepdims=False).astype(jnp.float32)
        * row_live[:, None]
    )
    matrices = [None] * layer_count
    columns = [None] * layer_count
    rowwise = [None] * layer_count
    for layer in reversed(range(layer_count)):
        upstream, matrices[layer], columns[layer], rowwise[layer] = layer_backward(
            upstream, saved[layer], layer_weights[layer], layer_small[layer], length
        )
    block_output = lax.all_gather(running.astype(jnp.bfloat16), "section", axis=0)
    half_width = model_width // layer_count
    low_grad = upstream.astype(jnp.bfloat16).reshape(row_count, layer_count, half_width)
    input_grad = lax.all_to_all(low_grad.transpose(1, 0, 2), "section", 0, 0)
    matrix = lax.psum_scatter(
        jnp.concatenate(matrices), ("section", "dp"), scatter_dimension=0, tiled=True
    ).astype(jnp.float32)
    up_share, down_share, qkv_share, out_share = jnp.split(matrix, cuts, axis=1)
    row_total = lax.psum(jnp.stack(rowwise), ("section", "dp", "tensor"))
    column_total = lax.psum(jnp.stack(columns), ("section", "dp"))
    row_mine = lax.dynamic_index_in_dim(row_total, section_index, 0, keepdims=False)
    row_mine = row_mine.reshape(6, -1, model_width // (dp_count * lax.axis_size("tensor")))
    row_mine = lax.dynamic_index_in_dim(
        row_mine, dp_index * lax.axis_size("tensor") + tensor_index, 1, keepdims=False
    )
    column_mine = lax.dynamic_index_in_dim(column_total, section_index, 0, keepdims=False)
    qv_mine = column_mine[: 2 * head_width].reshape(2, dp_count, -1)
    up_mine = column_mine[2 * head_width :].reshape(dp_count, -1)
    qv_mine = lax.dynamic_index_in_dim(qv_mine, dp_index, 1, keepdims=False)
    up_mine = lax.dynamic_index_in_dim(up_mine, dp_index, 0, keepdims=False)
    return (
        block_output,
        input_grad,
        qkv_share.reshape(1, -1, 3, head_width),
        qv_mine[None],
        out_share.T[None],
        row_mine[0][None],
        row_mine[1][None],
        row_mine[2][None],
        up_share[None],
        up_mine[None],
        down_share.T[None],
        row_mine[3][None],
        row_mine[4][None],
        row_mine[5][None],
    )


def solution(mesh):
    placed = (
        P("dp", "tensor", None),
        P("dp", "tensor", None),
        P("dp"),
        P("section", "dp", None, "tensor"),
        P("section", None, "tensor"),
        P("section", "tensor", "dp"),
        P("section", None),
        P("section", None),
        P("section", None),
        P("section", "dp", "tensor"),
        P("section", "tensor"),
        P("section", "tensor", "dp"),
        P("section", None),
        P("section", None),
        P("section", None),
    )
    return jax.shard_map(
        local,
        mesh=mesh,
        in_specs=placed,
        out_specs=(
            P("dp", "tensor", None),
            P("dp", "tensor", "section"),
            P("section", "dp", None, "tensor"),
            P("section", None, ("tensor", "dp")),
            P("section", "tensor", "dp"),
            P("section", ("dp", "tensor")),
            P("section", ("dp", "tensor")),
            P("section", ("dp", "tensor")),
            P("section", "dp", "tensor"),
            P("section", ("tensor", "dp")),
            P("section", "tensor", "dp"),
            P("section", ("dp", "tensor")),
            P("section", ("dp", "tensor")),
            P("section", ("dp", "tensor")),
        ),
        check_vma=False,
    )
```

```python
import functools

import jax
import jax.numpy as jnp
from jax import lax
from jax.experimental import pallas as pl
from jax.experimental.pallas import tpu as pltpu
from jax.sharding import PartitionSpec as P

HEAD_DIM = 64


masked_score = -1e30
norm_epsilon = 1e-05


def meet_peers(axis):
    me = lax.axis_index(axis)
    count = lax.axis_size(axis)
    barrier = pltpu.get_barrier_semaphore()
    for step in range(1, count):
        pl.semaphore_signal(
            barrier,
            inc=1,
            device_id={axis: lax.rem(me + step, count)},
            device_id_type=pl.DeviceIdType.MESH,
        )
    pl.semaphore_wait(barrier, count - 1)


def gather_kernel(axis, tile_ref, out_ref, send_sem, recv_sem):
    me = lax.axis_index(axis)
    count = lax.axis_size(axis)
    meet_peers(axis)
    copies = []
    for step in range(1, count):
        copy = pltpu.make_async_remote_copy(
            src_ref=tile_ref,
            dst_ref=out_ref.at[me],
            send_sem=send_sem.at[step],
            recv_sem=recv_sem.at[step],
            device_id={axis: lax.rem(me + step, count)},
            device_id_type=pl.DeviceIdType.MESH,
        )
        copy.start()
        copies.append(copy)
    out_ref[me] = tile_ref[...]
    for copy in copies:
        copy.wait()


def reduce_kernel(axis, partial_ref, out_ref, staged, landed, send_sem, recv_sem):
    me = lax.axis_index(axis)
    count = lax.axis_size(axis)
    staged[...] = partial_ref[...].astype(jnp.bfloat16)
    meet_peers(axis)
    copies = []
    for step in range(1, count):
        peer = lax.rem(me + step, count)
        copy = pltpu.make_async_remote_copy(
            src_ref=staged.at[peer],
            dst_ref=landed.at[step],
            send_sem=send_sem.at[step],
            recv_sem=recv_sem.at[step],
            device_id={axis: peer},
            device_id_type=pl.DeviceIdType.MESH,
        )
        copy.start()
        copies.append(copy)
    total = partial_ref[me]
    for step, copy in enumerate(copies):
        copy.wait()
        total = total + landed[step + 1].astype(jnp.float32)
    out_ref[...] = total


def gather_rows(tile):
    count = lax.axis_size("tensor")
    rows, width = tile.shape
    gathered = pl.pallas_call(
        functools.partial(gather_kernel, "tensor"),
        out_shape=jax.ShapeDtypeStruct((count, rows, width), tile.dtype),
        in_specs=[pl.BlockSpec(memory_space=pltpu.VMEM)],
        out_specs=pl.BlockSpec(memory_space=pltpu.VMEM),
        scratch_shapes=[
            pltpu.SemaphoreType.DMA((count,)),
            pltpu.SemaphoreType.DMA((count,)),
        ],
        compiler_params=pltpu.CompilerParams(
            collective_id=0, has_side_effects=True, vmem_limit_bytes=32 * 1024 * 1024
        ),
    )(tile)
    return gathered.reshape(count * rows, width)


def reduce_rows(partial_value):
    count = lax.axis_size("tensor")
    rows, width = partial_value.shape
    rows = rows // count
    return pl.pallas_call(
        functools.partial(reduce_kernel, "tensor"),
        out_shape=jax.ShapeDtypeStruct((rows, width), jnp.float32),
        in_specs=[pl.BlockSpec(memory_space=pltpu.VMEM)],
        out_specs=pl.BlockSpec(memory_space=pltpu.VMEM),
        scratch_shapes=[
            pltpu.VMEM((count, rows, width), jnp.bfloat16),
            pltpu.VMEM((count, rows, width), jnp.bfloat16),
            pltpu.SemaphoreType.DMA((count,)),
            pltpu.SemaphoreType.DMA((count,)),
        ],
        compiler_params=pltpu.CompilerParams(
            collective_id=1, has_side_effects=True, vmem_limit_bytes=32 * 1024 * 1024
        ),
    )(partial_value.reshape(count, rows, width))


gather_grads = gather_rows
reduce_grads = reduce_rows


def norm_forward(summed, gain, shift):
    centre = jnp.mean(summed, axis=-1, keepdims=True)
    centred = summed - centre
    inverse = lax.rsqrt(jnp.mean(centred * centred, axis=-1, keepdims=True) + norm_epsilon)
    scaled = centred * inverse
    return (scaled * gain + shift, scaled, inverse)


def norm_backward(upstream, scaled, inverse, gain):
    weighted = upstream * gain
    inner_sum = jnp.mean(weighted, axis=-1, keepdims=True)
    along_sum = jnp.mean(weighted * scaled, axis=-1, keepdims=True)
    return (
        inverse * (weighted - inner_sum - scaled * along_sum),
        jnp.sum(upstream * scaled, axis=0),
        jnp.sum(upstream, axis=0),
    )


def gelu_slope(hidden_pre):
    cumulative = 0.5 * (1.0 + lax.erf(hidden_pre * 0.7071067811865476))
    density = jnp.exp(-0.5 * hidden_pre * hidden_pre) * 0.3989422804014327
    return cumulative + hidden_pre * density


def masked_scores(queries, key_rows, length, score_scale):
    raw_scores = (
        jnp.einsum("qhd,khd->hqk", queries, key_rows, preferred_element_type=jnp.float32)
        * score_scale
    )
    key_live = jnp.arange(key_rows.shape[0]) < length
    return jnp.where(key_live[None, None, :], raw_scores, masked_score)


def layer_forward(incoming, full_weights, small_params, length):
    up_full, down_turned, qkv_full, out_turned = full_weights
    qv_bias, out_bias, gain_one, shift_one, up_bias, down_bias, gain_two, shift_two = small_params
    gathered = gather_rows(incoming.astype(jnp.bfloat16))
    seq_len, model_width = gathered.shape
    local_width = out_turned.shape[-1]
    head_count = local_width // HEAD_DIM
    score_scale = HEAD_DIM ** (-0.5)
    pre_proj = jnp.dot(
        gathered, qkv_full, preferred_element_type=jnp.float32
    )
    qkv_bias = jnp.stack([qv_bias[0], jnp.zeros_like(qv_bias[0]), qv_bias[1]]).reshape(
        3 * local_width
    )
    projected = (pre_proj + qkv_bias).astype(jnp.bfloat16).reshape(seq_len, 3, head_count, HEAD_DIM)
    raw_scores = masked_scores(projected[:, 0], projected[:, 1], length, score_scale)
    row_max = jnp.max(raw_scores, axis=-1, keepdims=True)
    exponent = jnp.exp(raw_scores - row_max)
    row_total = jnp.sum(exponent, axis=-1, keepdims=True)
    attn_probs = (exponent / row_total).astype(jnp.bfloat16)
    log_total = row_max + jnp.log(row_total)
    context = jnp.einsum(
        "hqk,khd->qhd", attn_probs, projected[:, 2], preferred_element_type=jnp.float32
    )
    context = context.reshape(seq_len, local_width).astype(jnp.bfloat16)
    attended = reduce_rows(jnp.einsum("sc,dc->sd", context, out_turned, preferred_element_type=jnp.float32))
    first_sum = incoming + attended + out_bias
    normed, scaled_one, inverse_one = norm_forward(first_sum, gain_one, shift_one)
    normed_rows = gather_rows(normed.astype(jnp.bfloat16))
    hidden_pre = jnp.dot(normed_rows, up_full, preferred_element_type=jnp.float32) + up_bias
    hidden = jax.nn.gelu(hidden_pre, approximate=False).astype(jnp.bfloat16)
    mlp_out = reduce_rows(jnp.einsum("sf,df->sd", hidden, down_turned, preferred_element_type=jnp.float32))
    second_sum = normed + mlp_out + down_bias
    result, scaled_two, inverse_two = norm_forward(second_sum, gain_two, shift_two)
    saved_acts = (
        gathered,
        projected,
        log_total,
        context,
        scaled_one,
        inverse_one,
        normed_rows,
        hidden_pre,
        hidden,
        scaled_two,
        inverse_two,
    )
    return (result, saved_acts)


def layer_backward(upstream, saved_acts, full_weights, small_params, length):
    (
        gathered,
        projected,
        log_total,
        context,
        scaled_one,
        inverse_one,
        normed_rows,
        hidden_pre,
        hidden,
        scaled_two,
        inverse_two,
    ) = saved_acts
    up_full, down_turned, qkv_full, out_turned = full_weights
    qv_bias, out_bias, gain_one, shift_one, up_bias, down_bias, gain_two, shift_two = small_params
    seq_len, model_width = gathered.shape
    local_width = out_turned.shape[-1]
    head_count = local_width // HEAD_DIM
    score_scale = HEAD_DIM ** (-0.5)
    second_grad, gain_two_grad, shift_two_grad = norm_backward(
        upstream, scaled_two, inverse_two, gain_two
    )
    down_bias_grad = jnp.sum(second_grad, axis=0)
    mixed_rows = gather_grads(second_grad.astype(jnp.bfloat16))
    down_grad = jnp.einsum("sf,sd->df", hidden, mixed_rows, preferred_element_type=jnp.float32)
    hidden_grad = jnp.einsum("sd,df->sf", mixed_rows, down_turned, preferred_element_type=jnp.float32)
    pre_grad = (hidden_grad * gelu_slope(hidden_pre)).astype(jnp.bfloat16)
    up_bias_grad = jnp.sum(pre_grad.astype(jnp.float32), axis=0)
    up_grad = jnp.einsum("sd,sf->df", normed_rows, pre_grad, preferred_element_type=jnp.float32)
    normed_grad = second_grad + reduce_grads(
        jnp.einsum("sf,df->sd", pre_grad, up_full, preferred_element_type=jnp.float32)
    )
    first_grad, gain_one_grad, shift_one_grad = norm_backward(
        normed_grad, scaled_one, inverse_one, gain_one
    )
    out_bias_grad = jnp.sum(first_grad, axis=0)
    attended_rows = gather_grads(first_grad.astype(jnp.bfloat16))
    out_grad = jnp.einsum("sc,sd->dc", context, attended_rows, preferred_element_type=jnp.float32)
    context_grad = jnp.einsum(
        "sd,dc->sc", attended_rows, out_turned, preferred_element_type=jnp.float32
    )
    context_grad = context_grad.astype(jnp.bfloat16).reshape(seq_len, head_count, HEAD_DIM)
    queries = projected[:, 0]
    key_rows = projected[:, 1]
    values = projected[:, 2]
    attn_probs = jnp.exp(masked_scores(queries, key_rows, length, score_scale) - log_total)
    value_grad = jnp.einsum(
        "hqk,qhd->khd",
        attn_probs.astype(jnp.bfloat16),
        context_grad,
        preferred_element_type=jnp.float32,
    )
    probs_grad = jnp.einsum(
        "qhd,khd->hqk", context_grad, values, preferred_element_type=jnp.float32
    )
    inner_sum = jnp.sum(attn_probs * probs_grad, axis=-1, keepdims=True)
    score_grad = (attn_probs * (probs_grad - inner_sum)).astype(jnp.bfloat16)
    query_grad = (
        jnp.einsum("hqk,khd->qhd", score_grad, key_rows, preferred_element_type=jnp.float32)
        * score_scale
    )
    key_grad = (
        jnp.einsum("hqk,qhd->khd", score_grad, queries, preferred_element_type=jnp.float32)
        * score_scale
    )
    proj_grad = (
        jnp.stack([query_grad, key_grad, value_grad], axis=1)
        .astype(jnp.bfloat16)
        .reshape(seq_len, 3 * local_width)
    )
    summed_proj = jnp.sum(proj_grad.astype(jnp.float32).reshape(seq_len, 3, local_width), axis=0)
    qv_bias_grad = jnp.stack([summed_proj[0], summed_proj[2]])
    qkv_grad = jnp.einsum(
        "sd,sx->dx", gathered, proj_grad, preferred_element_type=jnp.float32
    )
    input_part = jnp.einsum(
        "sx,dx->sd",
        proj_grad,
        qkv_full,
        preferred_element_type=jnp.float32,
    )
    input_grad = first_grad + reduce_grads(input_part)
    matrix = jnp.concatenate([up_grad, down_grad, qkv_grad, out_grad], axis=1).astype(jnp.bfloat16)
    columns = jnp.concatenate([qv_bias_grad.reshape(-1), up_bias_grad])
    rowwise = (
        out_bias_grad,
        gain_one_grad,
        shift_one_grad,
        down_bias_grad,
        gain_two_grad,
        shift_two_grad,
    )
    return (input_grad, matrix, columns, jnp.concatenate(rowwise))


def local(
    block_input,
    cotangent,
    lengths,
    qkv_weight,
    qv_bias,
    out_weight,
    out_bias,
    norm1_gain,
    norm1_bias,
    up_weight,
    up_bias,
    down_weight,
    down_bias,
    norm2_gain,
    norm2_bias,
):
    section_index = lax.axis_index("section")
    tensor_index = lax.axis_index("tensor")
    dp_index = lax.axis_index("dp")
    dp_count = lax.axis_size("dp")
    layer_count = lax.axis_size("section")
    row_count = block_input.shape[1]
    model_width = block_input.shape[2]
    head_width = out_weight.shape[1]
    hidden_width = up_weight.shape[2]
    length = lengths[section_index]
    row_live = tensor_index * row_count + jnp.arange(row_count) < length
    packed = jnp.concatenate(
        [
            up_weight[0],
            down_weight[0].T,
            qkv_weight[0].reshape(qkv_weight.shape[1], 3 * head_width),
            out_weight[0].T,
        ],
        axis=1,
    )
    cuts = [hidden_width, 2 * hidden_width, 2 * hidden_width + 3 * head_width]
    packed_full = lax.all_gather(packed, ("section", "dp"), axis=0, tiled=True)
    small = (qv_bias, out_bias, norm1_gain, norm1_bias, up_bias, down_bias, norm2_gain, norm2_bias)
    small_flat = jnp.concatenate([member.reshape(-1) for member in small])
    small_both = lax.all_gather(small_flat, "section", axis=0)
    layer_weights = []
    layer_small = []
    for layer in range(layer_count):
        whole = packed_full[layer * model_width : (layer + 1) * model_width]
        layer_weights.append(jnp.split(whole, cuts, axis=1))
        start = 0
        members = []
        for member in small:
            members.append(small_both[layer, start : start + member.size].reshape(member.shape[1:]))
            start += member.size
        layer_small.append(tuple(members))
    running = lax.dynamic_index_in_dim(block_input, section_index, 0, keepdims=False).astype(
        jnp.float32
    )
    saved = []
    for layer in range(layer_count):
        running, acts = layer_forward(running, layer_weights[layer], layer_small[layer], length)
        saved.append(acts)
    upstream = (
        lax.dynamic_index_in_dim(cotangent, section_index, 0, keepdims=False).astype(jnp.float32)
        * row_live[:, None]
    )
    matrices = [None] * layer_count
    columns = [None] * layer_count
    rowwise = [None] * layer_count
    for layer in reversed(range(layer_count)):
        upstream, matrices[layer], columns[layer], rowwise[layer] = layer_backward(
            upstream, saved[layer], layer_weights[layer], layer_small[layer], length
        )
    block_output = lax.all_gather(running.astype(jnp.bfloat16), "section", axis=0)
    half_width = model_width // layer_count
    low_grad = upstream.astype(jnp.bfloat16).reshape(row_count, layer_count, half_width)
    input_grad = lax.all_to_all(low_grad.transpose(1, 0, 2), "section", 0, 0)
    matrix = lax.psum_scatter(
        jnp.concatenate(matrices), ("section", "dp"), scatter_dimension=0, tiled=True
    ).astype(jnp.float32)
    up_share, down_share, qkv_share, out_share = jnp.split(matrix, cuts, axis=1)
    tensor_count = lax.axis_size("tensor")
    own_slot = jnp.arange(tensor_count)[None, :, None] == tensor_index
    column_slots = jnp.where(own_slot, jnp.stack(columns)[:, None, :], 0.0)
    vector_total = lax.psum(
        jnp.concatenate([jnp.stack(rowwise), column_slots.reshape(layer_count, -1)], axis=1),
        ("section", "dp", "tensor"),
    )
    row_total = vector_total[:, : 6 * model_width]
    column_total = lax.dynamic_index_in_dim(
        vector_total[:, 6 * model_width :].reshape(layer_count, tensor_count, -1),
        tensor_index,
        1,
        keepdims=False,
    )
    row_mine = lax.dynamic_index_in_dim(row_total, section_index, 0, keepdims=False)
    row_mine = row_mine.reshape(6, -1, model_width // (dp_count * lax.axis_size("tensor")))
    row_mine = lax.dynamic_index_in_dim(
        row_mine, dp_index * lax.axis_size("tensor") + tensor_index, 1, keepdims=False
    )
    column_mine = lax.dynamic_index_in_dim(column_total, section_index, 0, keepdims=False)
    qv_mine = column_mine[: 2 * head_width].reshape(2, dp_count, -1)
    up_mine = column_mine[2 * head_width :].reshape(dp_count, -1)
    qv_mine = lax.dynamic_index_in_dim(qv_mine, dp_index, 1, keepdims=False)
    up_mine = lax.dynamic_index_in_dim(up_mine, dp_index, 0, keepdims=False)
    return (
        block_output,
        input_grad,
        qkv_share.reshape(1, -1, 3, head_width),
        qv_mine[None],
        out_share.T[None],
        row_mine[0][None],
        row_mine[1][None],
        row_mine[2][None],
        up_share[None],
        up_mine[None],
        down_share.T[None],
        row_mine[3][None],
        row_mine[4][None],
        row_mine[5][None],
    )


def solution(mesh):
    placed = (
        P("dp", "tensor", None),
        P("dp", "tensor", None),
        P("dp"),
        P("section", "dp", None, "tensor"),
        P("section", None, "tensor"),
        P("section", "tensor", "dp"),
        P("section", None),
        P("section", None),
        P("section", None),
        P("section", "dp", "tensor"),
        P("section", "tensor"),
        P("section", "tensor", "dp"),
        P("section", None),
        P("section", None),
        P("section", None),
    )
    return jax.shard_map(
        local,
        mesh=mesh,
        in_specs=placed,
        out_specs=(
            P("dp", "tensor", None),
            P("dp", "tensor", "section"),
            P("section", "dp", None, "tensor"),
            P("section", None, ("tensor", "dp")),
            P("section", "tensor", "dp"),
            P("section", ("dp", "tensor")),
            P("section", ("dp", "tensor")),
            P("section", ("dp", "tensor")),
            P("section", "dp", "tensor"),
            P("section", ("tensor", "dp")),
            P("section", "tensor", "dp"),
            P("section", ("dp", "tensor")),
            P("section", ("dp", "tensor")),
            P("section", ("dp", "tensor")),
        ),
        check_vma=False,
    )
```
